32 devices in a mesh: head: 2 (over x), wide: 16 (over z, y, core).
Axes of the slice: x: 2, y: 2, z: 4, core: 2. Of those that a mesh axis runs over, the one named last changes fastest.
Arguments:
- queries: bfloat16 [4096, 2048], P('wide', 'head'), may hold values from -120 to 120
- keys: bfloat16 [4096, 2048], P('wide', 'head'), may hold values from -6 to 6
- values: bfloat16 [4096, 2048], P('wide', 'head'), may hold values from -6 to 6
- out_grad: bfloat16 [4096, 2048], P('wide', 'head'), may hold values from -6 to 6
- qkv_weight: bfloat16 [3, 4096, 2048], P(None, 'wide', 'head'), may hold values from -0.125 to 0.125
- doc_lengths: int32 [8], replicated, may hold values from 1 to 1023, as said below
- image_count: int32 [16], replicated, may hold values 0 or 1
- image_offset: int32 [16], replicated, may hold values from 0 to 192
- slab_owner: int32 [16], replicated, may hold values from 0 to 15, each once
- patch_weight: bfloat16 [256, 4096], P(None, 'head'), may hold values from -0.09375 to 0.09375
- conv_input: bfloat16 [16, 8, 8, 128], P('wide', 'head'), may hold values from -20 to 20
- pre_act: bfloat16 [16, 8, 8, 128], P('wide', 'head'), may hold values from -6 to 6
- kernel_first: float32 [1152, 128], P('wide'), may hold values from -0.1875 to 0.1875
- kernel_second: float32 [1152, 256], P('wide'), may hold values from -0.1875 to 0.1875
- mean_first: float32 [1152, 128], P('wide'), may hold values from -4 to 4
- mean_second: float32 [1152, 256], P('wide'), may hold values from -4 to 4
- square_first: float32 [1152, 128], P('wide'), may hold values from 0.05 to 1
- square_second: float32 [1152, 256], P('wide'), may hold values from 0.05 to 1
Outputs:
- input_grad_t: bfloat16 [4096, 4096], P('head', 'wide')
- new_kernel_first: float32 [1152, 128], P('wide')
- new_kernel_second: float32 [1152, 256], P('wide')
- new_mean_first: float32 [1152, 128], P('wide')
- new_mean_second: float32 [1152, 256], P('wide')
- new_square_first: float32 [1152, 128], P('wide')
- new_square_second: float32 [1152, 256], P('wide')
The draws below stay inside these ranges and needn't reach their ends.
Inputs may be any that keep to these rules, and one draw needn't show every extreme that they name: `doc_lengths`: the first document is longer than 256 and shorter than 768; the last has 1024 minus the first one's length; the documents between come in consecutive pairs whose lengths add up to 1024.
All inputs are finite; a program needn't handle non-finite values.
Results may differ from the reference program's by a relative error of at most 0.013.
Values may be sent and summed in bfloat16 or wider, within the bound.
A program may use at most 128 MiB of HBM per device.

```python
import math
import jax
import jax.numpy as jnp
from jax import lax

D = 4096
HEADS = 16
HD = 128
TOK_DEV = 256
REACH = 4
PROWS = 8
PCOLS = 8
PCH = 256
CMID = 128
CIN = 128
SEQ = 4096
DOCMAX = 1024
NDOC = 8
IMGTOK = 64
N_HEAD = 2
N_WIDE = 16


def paired_draw(key):
    folded_key = jax.random.fold_in(key, 31)
    first, second = jax.random.split(folded_key)
    width = HEADS * HD
    query = jnp.clip(jax.random.normal(first, (SEQ, width), jnp.float32), -6.0, 6.0)
    keyset = jnp.clip(jax.random.normal(second, (SEQ, width), jnp.float32), -6.0, 6.0)
    return (query, keyset)


def draw_queries(key, part):
    query, keyset = paired_draw(key)
    return query.astype(jnp.bfloat16)


def draw_keys(key, part):
    query, keyset = paired_draw(key)
    return keyset.astype(jnp.bfloat16)


def draw_doc_lengths(key, part):
    folded_key = jax.random.fold_in(key, 7)
    key_one, key_two, key_three = jax.random.split(folded_key, 3)
    pairs = NDOC // 2 - 1
    first = jax.random.randint(key_one, (1,), TOK_DEV + 1, DOCMAX - TOK_DEV, dtype=jnp.int32)
    shorter = jax.random.randint(key_two, (pairs,), 1, DOCMAX, dtype=jnp.int32)
    picked = jax.random.randint(key_three, (), 0, pairs, dtype=jnp.int32)
    shorter = jnp.where(jnp.arange(pairs, dtype=jnp.int32) == picked, 1, shorter)
    middle = jnp.stack([shorter, DOCMAX - shorter], axis=1).reshape(-1)
    return jnp.concatenate([first, middle, DOCMAX - first]).astype(jnp.int32)


def draw_conv_input(key, part):
    folded_key = jax.random.fold_in(key, 11)
    shape = (N_WIDE, PROWS, PCOLS, CIN)
    base = jnp.clip(jax.random.normal(folded_key, shape, jnp.float32), -6.0, 6.0)
    top = 3.2
    channel = jnp.arange(CIN, dtype=jnp.float32) / (CIN - 1)
    scale = jnp.exp(jnp.log(top) * channel)
    return (base * scale).astype(jnp.bfloat16)


def with_ends(entries, stream_key, smallest, high):
    spot = [jax.random.randint(jax.random.fold_in(stream_key, axis), (), 0, length) for axis, length in enumerate(entries.shape)]
    longest = entries.shape.index(max(entries.shape))
    neighbour = spot[:longest] + [(spot[longest] + 1) % entries.shape[longest]] + spot[longest + 1:]
    return entries.at[tuple(spot)].set(smallest).at[tuple(neighbour)].set(high)


def steps_of(own_key, shape, shards, least, high):
    def one(dim, parts):
        draws = jax.random.uniform(jax.random.fold_in(jax.random.fold_in(own_key, 6), dim), (parts,), jnp.float32, least / len(shards), high / len(shards))
        return jnp.repeat(jnp.exp(draws), shape[dim] // parts).reshape((-1,) + (1,) * (len(shape) - dim - 1))

    loudness = one(*shards[0])
    for cut in shards[1:]:
        loudness = loudness * one(*cut)
    return loudness


def centred(key, extent, deviation, most, shards=(), kind=jnp.bfloat16):
    gain = steps_of(key, extent, shards, -0.22, 0.18) if shards else 1.0
    values = jax.random.normal(key, extent, jnp.float32) * deviation * gain
    return jnp.minimum(jnp.maximum(values, -most), most).astype(kind)


def setup_inputs(seed: int = 0) -> dict:
    arg_keys = jax.random.split(jax.random.key(seed), 19)
    queries = draw_queries(jax.random.fold_in(arg_keys[18], 71), 0)
    keys = draw_keys(jax.random.fold_in(arg_keys[18], 71), 0)
    values = centred(arg_keys[2], (SEQ, HEADS * HD), 1.0, 6.0, ((0, 16), (1, 2)))
    out_grad = centred(arg_keys[3], (SEQ, HEADS * HD), 1.0, 6.0, ((0, 16), (1, 2)))
    qkv_weight = centred(arg_keys[4], (3, D, HEADS * HD), (HEADS * HD) ** -0.5, 0.125, ((1, 16), (2, 2)))
    doc_lengths = draw_doc_lengths(jax.random.fold_in(arg_keys[18], 71), 0)
    image_count = with_ends((jax.random.randint(arg_keys[6], (N_WIDE,), 0, 4) < 3).astype(jnp.int32), jax.random.fold_in(arg_keys[6], 1), 0, 1)
    image_offset = with_ends(jax.random.randint(arg_keys[7], (N_WIDE,), 0, TOK_DEV - IMGTOK + 1), jax.random.fold_in(arg_keys[7], 1), 0, TOK_DEV - IMGTOK).astype(jnp.int32)
    slab_owner = jax.random.permutation(arg_keys[8], N_WIDE).astype(jnp.int32)
    patch_weight = centred(arg_keys[9], (PCH, D), D ** -0.5, 0.09375, ((1, 2),))
    conv_input = draw_conv_input(jax.random.fold_in(arg_keys[18], 71), 0)
    pre_act = centred(arg_keys[11], (N_WIDE, PROWS, PCOLS, CMID), 1.0, 6.0, ((0, 16), (1, 2)))
    kernel_first = centred(arg_keys[12], (9 * CIN, CMID), (9 * CIN) ** -0.5, 0.1875, ((0, 16),), jnp.float32)
    kernel_second = centred(arg_keys[13], (9 * CMID, PCH), (9 * CMID) ** -0.5, 0.1875, ((0, 16),), jnp.float32)
    mean_first = centred(arg_keys[14], (9 * CIN, CMID), 0.3, 4.0, ((0, 16),), jnp.float32)
    mean_second = centred(arg_keys[15], (9 * CMID, PCH), 0.3, 4.0, ((0, 16),), jnp.float32)
    square_first = jnp.clip(jnp.exp(math.log(1.0) - 2.9957323 * jax.random.uniform(arg_keys[16], (9 * CIN, CMID), jnp.float32) ** steps_of(arg_keys[16], (9 * CIN, CMID), ((0, 16),), -0.2, 0.2)), 0.05, 1.0)
    square_second = jnp.clip(jnp.exp(math.log(1.0) - 2.9957323 * jax.random.uniform(arg_keys[17], (9 * CMID, PCH), jnp.float32) ** steps_of(arg_keys[17], (9 * CMID, PCH), ((0, 16),), -0.2, 0.2)), 0.05, 1.0)
    return {"queries": queries, "keys": keys, "values": values, "out_grad": out_grad, "qkv_weight": qkv_weight, "doc_lengths": doc_lengths, "image_count": image_count, "image_offset": image_offset, "slab_owner": slab_owner, "patch_weight": patch_weight, "conv_input": conv_input, "pre_act": pre_act, "kernel_first": kernel_first, "kernel_second": kernel_second, "mean_first": mean_first, "mean_second": mean_second, "square_first": square_first, "square_second": square_second}


neg_big = -1e+30
beta_one = 0.9
beta_two = 0.95
adam_eps = 1e-08
learn_rate = 0.02
decay_rate = 0.1
adam_step = 10
norm_eps = 1e-06

def lowered(value):
    return lax.optimization_barrier(value.astype(jnp.bfloat16)).astype(jnp.float32)

def doc_number(places, doc_lengths):
    ends = jnp.cumsum(doc_lengths)
    return lax.optimization_barrier(jnp.sum((places[:, None] >= ends[None, :]).astype(jnp.int32), axis=1))

def image_number(places, image_count, image_offset):
    safe = jnp.clip(places, 0, SEQ - 1)
    block = (safe // TOK_DEV).astype(jnp.int32)
    local = safe - block * TOK_DEV
    present = image_count[block]
    start = image_offset[block]
    inside = (present > 0) & (local >= start) & (local < start + IMGTOK) & (places >= 0)
    return jnp.where(inside, block, -1).astype(jnp.int32)

def allowed_mask(query_places, query_docs, query_images, key_places, key_docs, key_images):
    same_doc = query_docs[:, None] == key_docs[None, :]
    earlier = key_places[None, :] <= query_places[:, None]
    same_image = (query_images[:, None] == key_images[None, :]) & (query_images[:, None] >= 0)
    return same_doc & (earlier | same_image) & (key_places[None, :] >= 0)

def attend_block(query, key_all, value_all, grad_out, allowed):
    scale = 1.0 / math.sqrt(HD)
    rows = query.shape[0]
    count = key_all.shape[0]
    query_h = query.astype(jnp.float32).reshape(rows, -1, HD)
    key_h = key_all.astype(jnp.float32).reshape(count, -1, HD)
    value_h = value_all.astype(jnp.float32).reshape(count, -1, HD)
    grad_h = grad_out.astype(jnp.float32).reshape(rows, -1, HD)
    scores = jnp.einsum('qhd,khd->hqk', query_h, key_h) * scale
    scores = jnp.where(allowed[None], scores, neg_big)
    top = lax.optimization_barrier(jnp.max(scores, axis=-1, keepdims=True))
    expo = jnp.where(allowed[None], jnp.exp(scores - top), 0.0)
    prob = expo / lax.optimization_barrier(jnp.sum(expo, axis=-1, keepdims=True))
    prob_low = lowered(prob)
    output = jnp.einsum('hqk,khd->qhd', prob_low, value_h)
    delta = jnp.einsum('qhd,qhd->hq', grad_h, output)
    dprob = jnp.einsum('qhd,khd->hqk', grad_h, value_h)
    dscore = lowered(prob * (dprob - delta[:, :, None]))
    dquery = jnp.einsum('hqk,khd->qhd', dscore, key_h) * scale
    dkey = jnp.einsum('hqk,qhd->khd', dscore, query_h) * scale
    dvalue = jnp.einsum('hqk,qhd->khd', prob_low, grad_h)
    return (dquery.reshape(rows, -1), dkey.reshape(count, -1), dvalue.reshape(count, -1))

def adam_update(param, mean, square, grad):
    new_mean = beta_one * mean + (1.0 - beta_one) * grad
    new_square = beta_two * square + (1.0 - beta_two) * grad * grad
    fixed_mean = new_mean / (1.0 - beta_one ** adam_step)
    fixed_square = new_square / (1.0 - beta_two ** adam_step)
    new_param = param - learn_rate * (fixed_mean / (jnp.sqrt(fixed_square) + adam_eps) + decay_rate * param)
    return (new_param, new_mean, new_square)

def reference(queries, keys, values, out_grad, qkv_weight, doc_lengths, image_count, image_offset, slab_owner, patch_weight, conv_input, pre_act, kernel_first, kernel_second, mean_first, mean_second, square_first, square_second):
    head_width = HEADS * HD
    front = REACH * TOK_DEV
    window = (REACH + 1) * TOK_DEV
    places = jnp.arange(SEQ, dtype=jnp.int32)
    docs = doc_number(places, doc_lengths)
    images = image_number(places, image_count, image_offset)
    pad_places = jnp.arange(-front, SEQ, dtype=jnp.int32)
    pad_docs = jnp.concatenate([jnp.full((front,), -1, jnp.int32), docs])
    pad_images = jnp.concatenate([jnp.full((front,), -1, jnp.int32), images])
    zeros_front = jnp.zeros((front, head_width), jnp.bfloat16)
    pad_keys = jnp.concatenate([zeros_front, keys], axis=0)
    pad_values = jnp.concatenate([zeros_front, values], axis=0)

    def one_block(carry, block):
        key_acc, value_acc = carry
        begin = (block * TOK_DEV).astype(jnp.int32)
        query = lax.dynamic_slice_in_dim(queries, begin, TOK_DEV, 0)
        grad_out = lax.dynamic_slice_in_dim(out_grad, begin, TOK_DEV, 0)
        key_all = lax.dynamic_slice_in_dim(pad_keys, begin, window, 0)
        value_all = lax.dynamic_slice_in_dim(pad_values, begin, window, 0)
        allowed = allowed_mask(lax.dynamic_slice_in_dim(places, begin, TOK_DEV, 0), lax.dynamic_slice_in_dim(docs, begin, TOK_DEV, 0), lax.dynamic_slice_in_dim(images, begin, TOK_DEV, 0), lax.dynamic_slice_in_dim(pad_places, begin, window, 0), lax.dynamic_slice_in_dim(pad_docs, begin, window, 0), lax.dynamic_slice_in_dim(pad_images, begin, window, 0))
        dquery, dkey, dvalue = attend_block(query, key_all, value_all, grad_out, allowed)
        key_acc = lax.dynamic_update_slice_in_dim(key_acc, lax.dynamic_slice_in_dim(key_acc, begin, window, 0) + dkey, begin, 0)
        value_acc = lax.dynamic_update_slice_in_dim(value_acc, lax.dynamic_slice_in_dim(value_acc, begin, window, 0) + dvalue, begin, 0)
        return ((key_acc, value_acc), dquery)
    start_acc = jnp.zeros((front + SEQ, head_width), jnp.float32)
    (key_acc, value_acc), dqueries = lax.scan(one_block, (start_acc, start_acc), jnp.arange(N_WIDE, dtype=jnp.int32))
    grad_query = dqueries.reshape(SEQ, head_width).astype(jnp.bfloat16)
    grad_key = key_acc[front:].astype(jnp.bfloat16)
    grad_value = value_acc[front:].astype(jnp.bfloat16)
    grads = [grad_query, grad_key, grad_value]
    group_width = head_width // N_HEAD
    total = jnp.zeros((D, SEQ), jnp.float32)
    for group in range(N_HEAD):
        low_col = group * group_width
        partial_value = jnp.zeros((D, SEQ), jnp.float32)
        for proj in range(3):
            partial_value = partial_value + jnp.dot(qkv_weight[proj][:, low_col:low_col + group_width], grads[proj][:, low_col:low_col + group_width].T, preferred_element_type=jnp.float32)
        total = total + lowered(partial_value)
    input_grad_t = total.astype(jnp.bfloat16)
    patch_grad = lax.dot_general(input_grad_t, patch_weight, (((0,), (1,)), ((), ())), preferred_element_type=jnp.float32).astype(jnp.bfloat16)

    def take_image(block):
        begin = (block * TOK_DEV + image_offset[block]).astype(jnp.int32)
        return lax.dynamic_slice_in_dim(patch_grad, begin, IMGTOK, 0) * image_count[block].astype(jnp.bfloat16)
    segments = jax.vmap(take_image)(jnp.arange(N_WIDE, dtype=jnp.int32))
    incoming = jnp.zeros((N_WIDE, IMGTOK, PCH), jnp.bfloat16).at[slab_owner].set(segments)
    grad_img = incoming.astype(jnp.float32).reshape(N_WIDE, PROWS, PCOLS, PCH)
    act = lowered(jax.nn.silu(pre_act.astype(jnp.float32)))
    frame = ((0, 0), (1, 1), (1, 1), (0, 0))
    input_pad = jnp.pad(conv_input.astype(jnp.float32), frame)
    act_pad = jnp.pad(act, frame)
    grad_pad = jnp.pad(grad_img, frame)
    kernel_low = lowered(kernel_second).reshape(CMID, 9, PCH)
    second_list = []
    dact = jnp.zeros((N_WIDE, PROWS, PCOLS, CMID), jnp.float32)
    for row_shift in range(3):
        for col_shift in range(3):
            offset = row_shift * 3 + col_shift
            piece = act_pad[:, row_shift:row_shift + PROWS, col_shift:col_shift + PCOLS]
            second_list.append(jnp.einsum('nrcm,nrcp->mp', piece, grad_img))
            moved = grad_pad[:, 2 - row_shift:2 - row_shift + PROWS, 2 - col_shift:2 - col_shift + PCOLS]
            dact = dact + jnp.einsum('nrcp,mp->nrcm', moved, kernel_low[:, offset])
    grad_second = jnp.stack(second_list, axis=1).reshape(9 * CMID, PCH)
    pre_full = pre_act.astype(jnp.float32)
    sig = jax.nn.sigmoid(pre_full)
    dpre = lowered(dact * sig * (1.0 + pre_full * (1.0 - sig)))
    first_list = []
    for row_shift in range(3):
        for col_shift in range(3):
            piece = input_pad[:, row_shift:row_shift + PROWS, col_shift:col_shift + PCOLS]
            first_list.append(jnp.einsum('nrci,nrcm->im', piece, dpre))
    grad_first = jnp.stack(first_list, axis=1).reshape(9 * CIN, CMID)
    squares = jnp.sum(grad_first * grad_first) + jnp.sum(grad_second * grad_second)
    limit = 0.5 * math.sqrt(9 * CIN * CMID + 9 * CMID * PCH)
    factor = jnp.minimum(1.0, limit / (jnp.sqrt(squares) + norm_eps))
    kernel_one, mean_one, square_one = adam_update(kernel_first, mean_first, square_first, grad_first * factor)
    kernel_two, mean_two, square_two = adam_update(kernel_second, mean_second, square_second, grad_second * factor)
    return (input_grad_t, kernel_one, kernel_two, mean_one, mean_two, square_one, square_two)
```

```python
import functools
import math

import jax
import jax.numpy as jnp
from jax import lax
from jax.experimental import pallas as pl
from jax.experimental.pallas import tpu as pltpu
from jax.sharding import PartitionSpec as P

HD = 128
REACH = 4
PROWS = 8
PCOLS = 8
PCH = 256
CMID = 128
CIN = 128
IMGTOK = 64


neg_big = -1e30
beta_one = 0.9
beta_two = 0.95
adam_eps = 1e-08
learn_rate = 0.02
decay_rate = 0.1
adam_step = 10
norm_eps = 1e-06


def passed_along(block, axis, distance):
    devices = range(lax.axis_size(axis))
    route = [(i - distance, i) for i in devices if i - distance in devices]
    return lax.ppermute(block, axis, route)


def with_halo(cells, sides, width):
    for axis, dim in sides:
        count = lax.axis_size(axis)
        ends = count - 1
        head = lax.slice_in_dim(cells, 0, width, axis=dim)
        tail = lax.slice_in_dim(cells, cells.shape[dim] - width, cells.shape[dim], axis=dim)
        cells = jnp.concatenate(
            [
                lax.ppermute(tail, axis, [(i, (i + 1) % count) for i in range(ends)]),
                cells,
                lax.ppermute(head, axis, [((i + 1) % count, i) for i in range(ends)]),
            ],
            axis=dim,
        )
    return cells


def pick_entry(lookup, wanted):
    return jnp.sum(jnp.where(jnp.arange(lookup.shape[0]) == wanted, lookup, 0))


def doc_number(places, doc_lengths):
    ends = jnp.cumsum(doc_lengths)
    return jnp.sum((places[:, None] >= ends[None, :]).astype(jnp.int32), axis=1)


def image_number(block, local, image_count, image_offset):
    present = pick_entry(image_count, block)
    start = pick_entry(image_offset, block)
    inside = (present > 0) & (local >= start) & (local < start + IMGTOK)
    return jnp.where(inside, block, -1)


def allowed_mask(query_places, query_docs, query_images, key_places, key_docs, key_images):
    same_doc = query_docs[:, None] == key_docs[None, :]
    earlier = key_places[None, :] <= query_places[:, None]
    same_image = (query_images[:, None] == key_images[None, :]) & (query_images[:, None] >= 0)
    return same_doc & (earlier | same_image)


def attend_block(query, key_all, value_all, grad_out, allowed):
    scale = 1.0 / math.sqrt(HD)
    rows = query.shape[0]
    count = key_all.shape[0]
    query_h = query.reshape(rows, -1, HD)
    key_h = key_all.reshape(count, -1, HD)
    value_h = value_all.reshape(count, -1, HD)
    grad_h = grad_out.reshape(rows, -1, HD)
    scores = jnp.einsum("qhd,khd->hqk", query_h, key_h, preferred_element_type=jnp.float32) * scale
    scores = jnp.where(allowed[None], scores, neg_big)
    top = jnp.max(scores, axis=-1, keepdims=True)
    expo = jnp.where(allowed[None], jnp.exp(scores - top), 0.0)
    prob = expo / jnp.sum(expo, axis=-1, keepdims=True)
    prob_low = prob.astype(jnp.bfloat16)
    output = jnp.einsum("hqk,khd->qhd", prob_low, value_h, preferred_element_type=jnp.float32)
    delta = jnp.einsum("qhd,qhd->hq", grad_h.astype(jnp.float32), output)
    dprob = jnp.einsum("qhd,khd->hqk", grad_h, value_h, preferred_element_type=jnp.float32)
    dscore = (prob * (dprob - delta[:, :, None])).astype(jnp.bfloat16)
    dquery = jnp.einsum("hqk,khd->qhd", dscore, key_h, preferred_element_type=jnp.float32) * scale
    dkey = jnp.einsum("hqk,qhd->khd", dscore, query_h, preferred_element_type=jnp.float32) * scale
    dvalue = jnp.einsum("hqk,qhd->khd", prob_low, grad_h, preferred_element_type=jnp.float32)
    return (dquery.reshape(rows, -1), dkey.reshape(count, -1), dvalue.reshape(count, -1))


def adam_update(param, mean, square, grad):
    new_mean = beta_one * mean + (1.0 - beta_one) * grad
    new_square = beta_two * square + (1.0 - beta_two) * grad * grad
    fixed_mean = new_mean / (1.0 - beta_one**adam_step)
    fixed_square = new_square / (1.0 - beta_two**adam_step)
    new_param = param - learn_rate * (
        fixed_mean / (jnp.sqrt(fixed_square) + adam_eps) + decay_rate * param
    )
    return (new_param, new_mean, new_square)


def window_start(place, reach):
    return max(place, 1) - reach if place <= reach - 2 else 1


def attend_kernel(reach, x_ref, prev_ref, key_doc, key_img, query_doc, query_img, dq_ref, dkv_ref,
                  back_ref, keys, vals, dkeys, dvals):
    scale = 1.0 / math.sqrt(HD)
    rows = x_ref.shape[2]
    front = reach - 1
    for block in range(front):
        keys[block * rows : (block + 1) * rows] = prev_ref[block, 0]
        vals[block * rows : (block + 1) * rows] = prev_ref[block, 1]
    for block in range(reach):
        at = (front + block) * rows
        keys[at : at + rows] = x_ref[block, 1]
        vals[at : at + rows] = x_ref[block, 2]
    dkeys[...] = jnp.zeros_like(dkeys)
    dvals[...] = jnp.zeros_like(dvals)
    for place in range(reach):
        low = (front + window_start(place, reach)) * rows
        high = (front + place + 1) * rows
        query = x_ref[place, 0]
        grad_out = x_ref[place, 3]
        here = slice(place * rows, (place + 1) * rows)
        qdoc = query_doc[:, here]
        qimg = query_img[:, here]
        key_at = lax.broadcasted_iota(jnp.int32, (high - low, rows), 0) + low
        query_at = lax.broadcasted_iota(jnp.int32, (high - low, rows), 1) + (front + place) * rows
        allowed = (key_doc[low:high] == qdoc) & (
            (key_at <= query_at) | ((key_img[low:high] == qimg) & (qimg >= 0))
        )
        key = keys[low:high]
        across = (((1,), (1,)), ((), ()))
        scores = lax.dot_general(key, query, across, preferred_element_type=jnp.float32) * scale
        scores = jnp.where(allowed, scores, neg_big)
        expo = jnp.exp(scores - jnp.max(scores, axis=0, keepdims=True))
        prob = expo * (1.0 / jnp.sum(expo, axis=0, keepdims=True))
        prob_low = prob.astype(jnp.bfloat16)
        dprob = lax.dot_general(vals[low:high], grad_out, across, preferred_element_type=jnp.float32)
        delta = jnp.sum(prob_low.astype(jnp.float32) * dprob, axis=0, keepdims=True)
        dscore = (prob * (dprob - delta)).astype(jnp.bfloat16)
        dq = lax.dot_general(
            dscore, key, (((0,), (0,)), ((), ())), preferred_element_type=jnp.float32
        )
        dq_ref[place] = (dq * scale).astype(jnp.bfloat16)
        dkeys[low:high] += jnp.dot(dscore, query, preferred_element_type=jnp.float32) * scale
        dvals[low:high] += jnp.dot(prob_low, grad_out, preferred_element_type=jnp.float32)
    for block in range(front):
        here = slice(block * rows, (block + 1) * rows)
        back_ref[block, 0] = dkeys[here].astype(jnp.bfloat16)
        back_ref[block, 1] = dvals[here].astype(jnp.bfloat16)
    for block in range(reach):
        here = slice((front + block) * rows, (front + block + 1) * rows)
        dkv_ref[block, 0] = dkeys[here]
        dkv_ref[block, 1] = dvals[here]


def attend_heads(queries, keys, values, out_grad, doc_lengths, image_count, image_offset):
    rows, width = queries.shape
    wide_count = lax.axis_size("wide")
    device_index = lax.axis_index("wide")
    reach = REACH
    front = reach - 1
    part = width // reach
    groups = [[g * reach + i for i in range(reach)] for g in range(wide_count // reach)]
    packed = jnp.stack([queries, keys, values, out_grad]).reshape(4, rows, reach, part)
    packed = packed.transpose(2, 0, 1, 3)
    mine = lax.all_to_all(
        packed, "wide", split_axis=0, concat_axis=0, tiled=True, axis_index_groups=groups
    )
    prev = passed_along(mine[1:, 1:3], "wide", reach)
    first_block = device_index // reach * reach - front
    place = first_block * rows + jnp.arange((front + reach) * rows, dtype=jnp.int32)
    block = place // rows
    present = jnp.zeros_like(place)
    start = jnp.zeros_like(place)
    for b in range(wide_count):
        present = jnp.where(block == b, image_count[b], present)
        start = jnp.where(block == b, image_offset[b], start)
    local = place - block * rows
    inside = (place >= 0) & (present > 0) & (local >= start) & (local < start + IMGTOK)
    image = jnp.where(inside, block, -1)
    doc = jnp.where(place >= 0, doc_number(place, doc_lengths), -1)
    total = (front + reach) * rows
    heads = part // HD

    def by_head(*lead):
        return pl.BlockSpec((*lead, rows, HD), lambda h: (0,) * (len(lead) + 1) + (h,))

    def same(shape):
        return pl.BlockSpec(shape, lambda h: (0, 0))

    dq, dkv, back = pl.pallas_call(
        functools.partial(attend_kernel, reach),
        grid=(heads,),
        in_specs=[
            by_head(reach, 4),
            by_head(front, 2),
            same((total, 1)),
            same((total, 1)),
            same((1, reach * rows)),
            same((1, reach * rows)),
        ],
        out_specs=[by_head(reach), by_head(reach, 2), by_head(front, 2)],
        out_shape=[
            jax.ShapeDtypeStruct((reach, rows, part), jnp.bfloat16),
            jax.ShapeDtypeStruct((reach, 2, rows, part), jnp.float32),
            jax.ShapeDtypeStruct((front, 2, rows, part), jnp.bfloat16),
        ],
        scratch_shapes=[
            pltpu.VMEM((total, HD), jnp.bfloat16),
            pltpu.VMEM((total, HD), jnp.bfloat16),
            pltpu.VMEM((total, HD), jnp.float32),
            pltpu.VMEM((total, HD), jnp.float32),
        ],
        compiler_params=pltpu.CompilerParams(vmem_limit_bytes=40 * 1024 * 1024),
        cost_estimate=pl.CostEstimate(
            flops=heads * 17 * rows * rows * HD * 10,
            bytes_accessed=total * part * 24,
            transcendentals=heads * 17 * rows * rows,
        ),
    )(
        mine,
        prev,
        doc[:, None],
        image[:, None],
        doc[None, front * rows :],
        image[None, front * rows :],
    )
    late = passed_along(back, "wide", -reach).astype(jnp.float32)
    dkv = jnp.concatenate([dkv[:1], dkv[1:] + late], axis=0).astype(jnp.bfloat16)
    grads = jnp.concatenate([dq[:, None], dkv], axis=1)
    grads = lax.all_to_all(
        grads, "wide", split_axis=0, concat_axis=0, tiled=True, axis_index_groups=groups
    )
    return grads.transpose(1, 2, 0, 3).reshape(3, rows, width)


def attend_ring(queries, keys, values, out_grad, doc_lengths, image_count, image_offset):
    tokens_here = queries.shape[0]
    wide_count = lax.axis_size("wide")
    device_index = lax.axis_index("wide")
    local_places = jnp.arange(tokens_here, dtype=jnp.int32)
    query_places = device_index * tokens_here + local_places
    query_docs = doc_number(query_places, doc_lengths)
    query_images = image_number(device_index, local_places, image_count, image_offset)
    own_block = jnp.stack([keys, values])
    blocks = [own_block]
    moving = own_block
    for offset in range(REACH):
        moving = passed_along(moving, "wide", 1)
        blocks.append(moving)
    masks = []
    for offset in range(REACH + 1):
        source = (device_index - offset) % wide_count
        key_places = source * tokens_here + local_places
        key_docs = doc_number(key_places, doc_lengths)
        key_images = image_number(source, local_places, image_count, image_offset)
        visible = allowed_mask(
            query_places, query_docs, query_images, key_places, key_docs, key_images
        )
        masks.append(visible & (device_index - offset >= 0))
    allowed = jnp.concatenate(masks, axis=1)
    key_all = jnp.concatenate([block[0] for block in blocks], axis=0)
    value_all = jnp.concatenate([block[1] for block in blocks], axis=0)
    dquery, dkey, dvalue = attend_block(queries, key_all, value_all, out_grad, allowed)
    parts = [
        jnp.stack(
            [
                dkey[offset * tokens_here : (offset + 1) * tokens_here],
                dvalue[offset * tokens_here : (offset + 1) * tokens_here],
            ]
        )
        for offset in range(REACH + 1)
    ]
    carried = jnp.zeros_like(parts[0])
    for offset in range(REACH):
        carried = passed_along(carried + parts[REACH - offset], "wide", -1)
    key_grads = parts[0] + carried
    return jnp.stack(
        [
            dquery.astype(jnp.bfloat16),
            key_grads[0].astype(jnp.bfloat16),
            key_grads[1].astype(jnp.bfloat16),
        ]
    )
def tail_kernel(slab_ref, seg_ref, klow_ref, act_t, in_t, pre_ref, kern1, kern2, mean1, mean2, sq1, sq2,
                o_k1, o_k2, o_m1, o_m2, o_s1, o_s2,
                seg_all, klow_all, out_seg, seg_in, grads, grads_in, total_all, norm_all,
                sem_hs, sem_hr, sem_ks, sem_kr, sem_ss, sem_sr, sem_gs, sem_gr, sem_ts, sem_tr, sem_ns, sem_nr):
    heads, wide = seg_all.shape[0], klow_all.shape[0]
    me, head = lax.axis_index("wide"), lax.axis_index("head")
    slab = pre_ref.shape[0]
    send_rows = out_seg.shape[0]
    pad = klow_all.shape[1]
    chunk = kern1.shape[0]

    def go(axis, mine, count, source, dest, send, recv):
        def one(d, c):
            peer = lax.rem(mine + d, count)
            pltpu.make_async_remote_copy(
                src_ref=source(peer), dst_ref=dest.at[mine], send_sem=send.at[peer],
                recv_sem=recv.at[mine], device_id={axis: peer},
                device_id_type=pl.DeviceIdType.MESH,
            ).start()
            return c

        lax.fori_loop(1, count, one, 0)

    def done(axis, mine, count, source, dest, send, recv):
        def one(d, c):
            peer = lax.rem(mine + d, count)
            copy = pltpu.make_async_remote_copy(
                src_ref=source(peer), dst_ref=dest.at[peer], send_sem=send.at[peer],
                recv_sem=recv.at[peer], device_id={axis: peer},
                device_id_type=pl.DeviceIdType.MESH,
            )
            copy.wait_send()
            copy.wait_recv()
            return c

        lax.fori_loop(1, count, one, 0)

    barrier = pltpu.get_barrier_semaphore()

    def hello(axis, mine, count):
        def one(d, c):
            pl.semaphore_signal(barrier, inc=1, device_id={axis: lax.rem(mine + d, count)},
                                device_id_type=pl.DeviceIdType.MESH)
            return c

        lax.fori_loop(1, count, one, 0)

    hello("head", head, heads)
    hello("wide", me, wide)
    pl.semaphore_wait(barrier, heads + wide - 2)

    seg_all[head] = seg_ref[...]
    by_head = ("head", head, heads, lambda p: seg_all.at[head], seg_all, sem_hs, sem_hr)
    go(*by_head)
    klow_all[me] = klow_ref[...]
    by_kern = ("wide", me, wide, lambda p: klow_all.at[me], klow_all, sem_ks, sem_kr)
    go(*by_kern)
    done(*by_head)
    rows = pl.ds(pl.multiple_of(head * slab, 8), send_rows)
    seg = seg_all[0, rows]
    for h in range(1, heads):
        seg = seg + seg_all[h, rows]
    out_seg[...] = seg.astype(jnp.bfloat16)
    by_seg = ("wide", me, wide, lambda p: out_seg, seg_in, sem_ss, sem_sr)
    go(*by_seg)
    seg_in[me] = out_seg[...]
    done(*by_kern)
    cmid = pre_ref.shape[1]
    flat = klow_all[...].reshape(wide * pad, klow_all.shape[2])
    middle = chunk // 9
    row = lax.broadcasted_iota(jnp.int32, (cmid, wide * pad), 0)
    col = lax.broadcasted_iota(jnp.int32, (cmid, wide * pad), 1)
    place = row // middle * pad + row % middle * 9
    second = []
    for o in range(9):
        pick = (col == place + o).astype(jnp.float32).astype(jnp.bfloat16)
        second.append(
            jnp.dot(pick, flat, preferred_element_type=jnp.float32).astype(jnp.bfloat16)
        )
    done(*by_seg)
    incoming = jnp.zeros((send_rows, seg_in.shape[2]), jnp.float32)
    for n in range(wide):
        chosen = jnp.where(slab_ref[n] == me, 1.0, 0.0)
        incoming = incoming + seg_in[n].astype(jnp.float32) * chosen
    column = lax.broadcasted_iota(jnp.int32, incoming.shape, 0) % PCOLS
    shifted = [
        jnp.where(column < PCOLS - 1, pltpu.roll(incoming, send_rows - 1, 0), 0.0),
        incoming,
        jnp.where(column > 0, pltpu.roll(incoming, 1, 0), 0.0),
    ]
    dact = jnp.zeros((slab, cmid), jnp.float32)
    for o in range(9):
        start = PCOLS * (2 - o // 3)
        moved = shifted[o % 3][start : start + slab].astype(jnp.bfloat16)
        dact = dact + lax.dot_general(
            moved, second[o], (((1,), (1,)), ((), ())), preferred_element_type=jnp.float32
        )
    pre = pre_ref[...].astype(jnp.float32)
    sig = 1.0 / (1.0 + jnp.exp(-pre))
    dpre = (dact * sig * (1.0 + pre * (1.0 - sig))).astype(jnp.bfloat16)
    middle_in = incoming[PCOLS : PCOLS + slab].astype(jnp.bfloat16)
    width1 = dpre.shape[1]
    width2 = middle_in.shape[1]
    for w in range(wide):
        grads[w, :, :width1] = jnp.dot(
            in_t[w], dpre, preferred_element_type=jnp.float32
        ).astype(jnp.bfloat16)
        grads[w, :, width1:] = jnp.dot(
            act_t[w], middle_in, preferred_element_type=jnp.float32
        ).astype(jnp.bfloat16)
    by_grad = ("wide", me, wide, lambda p: grads.at[p], grads_in, sem_gs, sem_gr)
    go(*by_grad)
    grads_in[me] = grads[me]
    done(*by_grad)
    total = grads_in[0].astype(jnp.float32)
    for w in range(1, wide):
        total = total + grads_in[w].astype(jnp.float32)
    total_all[head] = total
    by_total = ("head", head, heads, lambda p: total_all.at[head], total_all, sem_ts, sem_tr)
    go(*by_total)
    done(*by_total)
    total = total_all[0]
    for h in range(1, heads):
        total = total + total_all[h]
    square = jnp.sum(total * total, axis=0, keepdims=True)
    square = jnp.sum(square, axis=1, keepdims=True)
    norm_all[me] = jnp.broadcast_to(square, norm_all.shape[1:])
    by_norm = ("wide", me, wide, lambda p: norm_all.at[me], norm_all, sem_ns, sem_nr)
    go(*by_norm)
    done(*by_norm)
    squares = norm_all[0]
    for w in range(1, wide):
        squares = squares + norm_all[w]
    squares = squares[:1, :1]
    limit = 0.5 * math.sqrt(wide * chunk * (width1 + width2))
    factor = jnp.minimum(1.0, limit / (jnp.sqrt(squares) + norm_eps))
    total = total * factor
    o_k1[...], o_m1[...], o_s1[...] = adam_update(
        kern1[...], mean1[...], sq1[...], total[:chunk, :width1]
    )
    o_k2[...], o_m2[...], o_s2[...] = adam_update(
        kern2[...], mean2[...], sq2[...], total[:chunk, width1:]
    )


def conv_update(seg, slab_owner, act, conv_input, pre_act, params):
    wide = lax.axis_size("wide")
    heads = lax.axis_size("head")
    slab_rows = pre_act.shape[1]
    slab = slab_rows * PCOLS
    kern1, kern2 = params[0], params[1]
    chunk = kern1.shape[0]
    pad = (chunk + 15) // 16 * 16
    send_rows = (slab + 2 * PCOLS + 15) // 16 * 16
    seg_rows = (heads - 1) * slab + send_rows
    seg = jnp.pad(seg, ((PCOLS, seg_rows - PCOLS - seg.shape[0]), (0, 0)))
    klow = jnp.pad(kern2.astype(jnp.bfloat16), ((0, pad - chunk), (0, 0)))
    both = with_halo(jnp.stack([conv_input, act]), (("head", 2),), 1)
    rims = jnp.pad(both, ((0, 0), (0, 0), (0, 0), (1, 1), (0, 0)))
    pieces = jnp.stack(
        [
            rims[:, 0, r : r + slab_rows, c : c + PCOLS].reshape(2, slab, -1)
            for r in range(3)
            for c in range(3)
        ],
        axis=1,
    )
    pieces = pieces.transpose(0, 3, 1, 2).reshape(2, wide, chunk, slab)
    pieces = jnp.pad(pieces, ((0, 0), (0, 0), (0, pad - chunk), (0, 0)))
    pch = kern2.shape[1]
    both_width = pch + kern1.shape[1]
    vmem = pl.BlockSpec(memory_space=pltpu.VMEM)
    dma = pltpu.SemaphoreType.DMA
    low, full = jnp.bfloat16, jnp.float32
    return pl.pallas_call(
        tail_kernel,
        in_specs=[pl.BlockSpec(memory_space=pltpu.SMEM)] + [vmem] * 11,
        out_specs=[vmem] * 6,
        out_shape=[jax.ShapeDtypeStruct(p.shape, p.dtype) for p in params],
        scratch_shapes=[
            pltpu.VMEM((heads, seg_rows, pch), full),
            pltpu.VMEM((wide, pad, pch), low),
            pltpu.VMEM((send_rows, pch), low),
            pltpu.VMEM((wide, send_rows, pch), low),
            pltpu.VMEM((wide, pad, both_width), low),
            pltpu.VMEM((wide, pad, both_width), low),
            pltpu.VMEM((heads, pad, both_width), full),
            pltpu.VMEM((wide, 8, 128), full),
        ]
        + [dma((n,)) for n in (heads, wide, wide, wide, heads, wide) for _ in range(2)],
        compiler_params=pltpu.CompilerParams(
            collective_id=0, has_side_effects=True, vmem_limit_bytes=32 * 1024 * 1024
        ),
        cost_estimate=pl.CostEstimate(
            flops=10**9, bytes_accessed=4 * 10**6, transcendentals=10**4
        ),
    )(slab_owner, seg, klow, pieces[1], pieces[0], pre_act.reshape(slab, -1), *params)


def shards(
    queries,
    keys,
    values,
    out_grad,
    qkv_weight,
    doc_lengths,
    image_count,
    image_offset,
    slab_owner,
    patch_weight,
    conv_input,
    pre_act,
    kernel_first,
    kernel_second,
    mean_first,
    mean_second,
    square_first,
    square_second,
):
    device_index = lax.axis_index("wide")
    heads_here = queries.shape[1] // HD
    wide_count = lax.axis_size("wide")
    split = heads_here % REACH == 0 and wide_count % REACH == 0
    grads = (attend_heads if split else attend_ring)(
        queries, keys, values, out_grad, doc_lengths, image_count, image_offset
    )
    partial_value = jnp.einsum(
        "prk,ptk->rt",
        lax.all_gather(qkv_weight, "wide", axis=1, tiled=True),
        grads,
        preferred_element_type=jnp.float32,
    ).astype(jnp.bfloat16)
    input_grad_t = (
        lax.psum_scatter(partial_value, "head", scatter_dimension=0, tiled=True)
        .astype(jnp.float32)
        .astype(jnp.bfloat16)
    )
    patch_part = lax.dot_general(
        input_grad_t, patch_weight, (((0,), (1,)), ((), ())), preferred_element_type=jnp.float32
    )
    has_image = pick_entry(image_count, device_index)
    offset_here = pick_entry(image_offset, device_index)
    segment = lax.dynamic_slice_in_dim(patch_part, offset_here, IMGTOK, 0)
    segment = segment * has_image.astype(jnp.float32)
    act = jax.nn.silu(pre_act.astype(jnp.float32)).astype(jnp.bfloat16)
    updated = conv_update(
        segment,
        slab_owner,
        act,
        conv_input,
        pre_act,
        (kernel_first, kernel_second, mean_first, mean_second, square_first, square_second),
    )
    kernel_one, kernel_two, mean_one, mean_two, square_one, square_two = updated
    return (input_grad_t, kernel_one, kernel_two, mean_one, mean_two, square_one, square_two)


def solution(mesh):
    in_specs = (
        P("wide", "head"),
        P("wide", "head"),
        P("wide", "head"),
        P("wide", "head"),
        P(None, "wide", "head"),
        P(),
        P(),
        P(),
        P(),
        P(None, "head"),
        P("wide", "head", None, None),
        P("wide", "head", None, None),
        P("wide", None),
        P("wide", None),
        P("wide", None),
        P("wide", None),
        P("wide", None),
        P("wide", None),
    )
    out_specs = (
        P("head", "wide"),
        P("wide", None),
        P("wide", None),
        P("wide", None),
        P("wide", None),
        P("wide", None),
        P("wide", None),
    )
    return jax.shard_map(shards, mesh=mesh, in_specs=in_specs, out_specs=out_specs, check_vma=False)
```

```python
import functools
import math

import jax
import jax.numpy as jnp
from jax import lax
from jax.experimental import pallas as pl
from jax.experimental.pallas import tpu as pltpu
from jax.sharding import PartitionSpec as P

HD = 128
REACH = 4
PROWS = 8
PCOLS = 8
PCH = 256
CMID = 128
CIN = 128
IMGTOK = 64


neg_big = -1e30
beta_one = 0.9
beta_two = 0.95
adam_eps = 1e-08
learn_rate = 0.02
decay_rate = 0.1
adam_step = 10
norm_eps = 1e-06


def passed_along(block, axis, distance):
    devices = range(lax.axis_size(axis))
    route = [(i - distance, i) for i in devices if i - distance in devices]
    return lax.ppermute(block, axis, route)


def with_halo(cells, sides, width):
    for axis, dim in sides:
        count = lax.axis_size(axis)
        ends = count - 1
        head = lax.slice_in_dim(cells, 0, width, axis=dim)
        tail = lax.slice_in_dim(cells, cells.shape[dim] - width, cells.shape[dim], axis=dim)
        cells = jnp.concatenate(
            [
                lax.ppermute(tail, axis, [(i, (i + 1) % count) for i in range(ends)]),
                cells,
                lax.ppermute(head, axis, [((i + 1) % count, i) for i in range(ends)]),
            ],
            axis=dim,
        )
    return cells


def pick_entry(lookup, wanted):
    return jnp.sum(jnp.where(jnp.arange(lookup.shape[0]) == wanted, lookup, 0))


def doc_number(places, doc_lengths):
    ends = jnp.cumsum(doc_lengths)
    return jnp.sum((places[:, None] >= ends[None, :]).astype(jnp.int32), axis=1)


def image_number(block, local, image_count, image_offset):
    present = pick_entry(image_count, block)
    start = pick_entry(image_offset, block)
    inside = (present > 0) & (local >= start) & (local < start + IMGTOK)
    return jnp.where(inside, block, -1)


def allowed_mask(query_places, query_docs, query_images, key_places, key_docs, key_images):
    same_doc = query_docs[:, None] == key_docs[None, :]
    earlier = key_places[None, :] <= query_places[:, None]
    same_image = (query_images[:, None] == key_images[None, :]) & (query_images[:, None] >= 0)
    return same_doc & (earlier | same_image)


def attend_block(query, key_all, value_all, grad_out, allowed):
    scale = 1.0 / math.sqrt(HD)
    rows = query.shape[0]
    count = key_all.shape[0]
    query_h = query.reshape(rows, -1, HD)
    key_h = key_all.reshape(count, -1, HD)
    value_h = value_all.reshape(count, -1, HD)
    grad_h = grad_out.reshape(rows, -1, HD)
    scores = jnp.einsum("qhd,khd->hqk", query_h, key_h, preferred_element_type=jnp.float32) * scale
    scores = jnp.where(allowed[None], scores, neg_big)
    top = jnp.max(scores, axis=-1, keepdims=True)
    expo = jnp.where(allowed[None], jnp.exp(scores - top), 0.0)
    prob = expo / jnp.sum(expo, axis=-1, keepdims=True)
    prob_low = prob.astype(jnp.bfloat16)
    output = jnp.einsum("hqk,khd->qhd", prob_low, value_h, preferred_element_type=jnp.float32)
    delta = jnp.einsum("qhd,qhd->hq", grad_h.astype(jnp.float32), output)
    dprob = jnp.einsum("qhd,khd->hqk", grad_h, value_h, preferred_element_type=jnp.float32)
    dscore = (prob * (dprob - delta[:, :, None])).astype(jnp.bfloat16)
    dquery = jnp.einsum("hqk,khd->qhd", dscore, key_h, preferred_element_type=jnp.float32) * scale
    dkey = jnp.einsum("hqk,qhd->khd", dscore, query_h, preferred_element_type=jnp.float32) * scale
    dvalue = jnp.einsum("hqk,qhd->khd", prob_low, grad_h, preferred_element_type=jnp.float32)
    return (dquery.reshape(rows, -1), dkey.reshape(count, -1), dvalue.reshape(count, -1))


def adam_update(param, mean, square, grad):
    new_mean = beta_one * mean + (1.0 - beta_one) * grad
    new_square = beta_two * square + (1.0 - beta_two) * grad * grad
    fixed_mean = new_mean / (1.0 - beta_one**adam_step)
    fixed_square = new_square / (1.0 - beta_two**adam_step)
    new_param = param - learn_rate * (
        fixed_mean / (jnp.sqrt(fixed_square) + adam_eps) + decay_rate * param
    )
    return (new_param, new_mean, new_square)


def window_start(place, reach):
    return max(place, 1) - reach if place <= reach - 2 else 1


def attend_kernel(reach, x_ref, prev_ref, key_doc, key_img, query_doc, query_img, dq_ref, dkv_ref,
                  back_ref, keys, vals, dkeys, dvals):
    scale = 1.0 / math.sqrt(HD)
    rows = x_ref.shape[2]
    front = reach - 1
    for block in range(front):
        keys[block * rows : (block + 1) * rows] = prev_ref[block, 0]
        vals[block * rows : (block + 1) * rows] = prev_ref[block, 1]
    for block in range(reach):
        at = (front + block) * rows
        keys[at : at + rows] = x_ref[block, 1]
        vals[at : at + rows] = x_ref[block, 2]
    dkeys[...] = jnp.zeros_like(dkeys)
    dvals[...] = jnp.zeros_like(dvals)
    for place in range(reach):
        low = (front + window_start(place, reach)) * rows
        high = (front + place + 1) * rows
        query = x_ref[place, 0]
        grad_out = x_ref[place, 3]
        here = slice(place * rows, (place + 1) * rows)
        qdoc = query_doc[:, here]
        qimg = query_img[:, here]
        key_at = lax.broadcasted_iota(jnp.int32, (high - low, rows), 0) + low
        query_at = lax.broadcasted_iota(jnp.int32, (high - low, rows), 1) + (front + place) * rows
        allowed = (key_doc[low:high] == qdoc) & (
            (key_at <= query_at) | ((key_img[low:high] == qimg) & (qimg >= 0))
        )
        key = keys[low:high]
        across = (((1,), (1,)), ((), ()))
        scores = lax.dot_general(key, query, across, preferred_element_type=jnp.float32) * scale
        scores = jnp.where(allowed, scores, neg_big)
        expo = jnp.exp(scores - jnp.max(scores, axis=0, keepdims=True))
        prob = expo * (1.0 / jnp.sum(expo, axis=0, keepdims=True))
        prob_low = prob.astype(jnp.bfloat16)
        dprob = lax.dot_general(vals[low:high], grad_out, across, preferred_element_type=jnp.float32)
        delta = jnp.sum(prob_low.astype(jnp.float32) * dprob, axis=0, keepdims=True)
        dscore = (prob * (dprob - delta)).astype(jnp.bfloat16)
        dq = lax.dot_general(
            dscore, key, (((0,), (0,)), ((), ())), preferred_element_type=jnp.float32
        )
        dq_ref[place] = (dq * scale).astype(jnp.bfloat16)
        dkeys[low:high] += jnp.dot(dscore, query, preferred_element_type=jnp.float32) * scale
        dvals[low:high] += jnp.dot(prob_low, grad_out, preferred_element_type=jnp.float32)
    for block in range(front):
        here = slice(block * rows, (block + 1) * rows)
        back_ref[block, 0] = dkeys[here].astype(jnp.bfloat16)
        back_ref[block, 1] = dvals[here].astype(jnp.bfloat16)
    for block in range(reach):
        here = slice((front + block) * rows, (front + block + 1) * rows)
        dkv_ref[block, 0] = dkeys[here]
        dkv_ref[block, 1] = dvals[here]


def attend_heads(queries, keys, values, out_grad, doc_lengths, image_count, image_offset):
    rows, width = queries.shape
    wide_count = lax.axis_size("wide")
    device_index = lax.axis_index("wide")
    reach = REACH
    front = reach - 1
    part = width // reach
    groups = [[g * reach + i for i in range(reach)] for g in range(wide_count // reach)]
    packed = jnp.stack([queries, keys, values, out_grad]).reshape(4, rows, reach, part)
    packed = packed.transpose(2, 0, 1, 3)
    mine = lax.all_to_all(
        packed, "wide", split_axis=0, concat_axis=0, tiled=True, axis_index_groups=groups
    )
    prev = passed_along(mine[1:, 1:3], "wide", reach)
    first_block = device_index // reach * reach - front
    place = first_block * rows + jnp.arange((front + reach) * rows, dtype=jnp.int32)
    block = place // rows
    present = jnp.zeros_like(place)
    start = jnp.zeros_like(place)
    for b in range(wide_count):
        present = jnp.where(block == b, image_count[b], present)
        start = jnp.where(block == b, image_offset[b], start)
    local = place - block * rows
    inside = (place >= 0) & (present > 0) & (local >= start) & (local < start + IMGTOK)
    image = jnp.where(inside, block, -1)
    ends = jnp.cumsum(doc_lengths)
    doc = jnp.where(place >= 0, 0, -1)
    for n in range(doc_lengths.shape[0]):
        doc = doc + (place >= ends[n]).astype(jnp.int32)
    doc, image = lax.optimization_barrier((doc, image))
    total = (front + reach) * rows
    heads = part // HD

    def by_head(*lead):
        return pl.BlockSpec((*lead, rows, HD), lambda h: (0,) * (len(lead) + 1) + (h,))

    def same(shape):
        return pl.BlockSpec(shape, lambda h: (0, 0))

    dq, dkv, back = pl.pallas_call(
        functools.partial(attend_kernel, reach),
        grid=(heads,),
        in_specs=[
            by_head(reach, 4),
            by_head(front, 2),
            same((total, 1)),
            same((total, 1)),
            same((1, reach * rows)),
            same((1, reach * rows)),
        ],
        out_specs=[by_head(reach), by_head(reach, 2), by_head(front, 2)],
        out_shape=[
            jax.ShapeDtypeStruct((reach, rows, part), jnp.bfloat16),
            jax.ShapeDtypeStruct((reach, 2, rows, part), jnp.float32),
            jax.ShapeDtypeStruct((front, 2, rows, part), jnp.bfloat16),
        ],
        scratch_shapes=[
            pltpu.VMEM((total, HD), jnp.bfloat16),
            pltpu.VMEM((total, HD), jnp.bfloat16),
            pltpu.VMEM((total, HD), jnp.float32),
            pltpu.VMEM((total, HD), jnp.float32),
        ],
        compiler_params=pltpu.CompilerParams(vmem_limit_bytes=40 * 1024 * 1024),
        cost_estimate=pl.CostEstimate(
            flops=heads * 17 * rows * rows * HD * 10,
            bytes_accessed=total * part * 24,
            transcendentals=heads * 17 * rows * rows,
        ),
    )(
        mine,
        prev,
        doc[:, None],
        image[:, None],
        doc[None, front * rows :],
        image[None, front * rows :],
    )
    late = passed_along(back, "wide", -reach).astype(jnp.float32)
    dkv = jnp.concatenate([dkv[:1], dkv[1:] + late], axis=0).astype(jnp.bfloat16)
    grads = jnp.concatenate([dq[:, None], dkv], axis=1)
    grads = lax.all_to_all(
        grads, "wide", split_axis=0, concat_axis=0, tiled=True, axis_index_groups=groups
    )
    return grads.transpose(1, 2, 0, 3).reshape(3, rows, width)


def attend_ring(queries, keys, values, out_grad, doc_lengths, image_count, image_offset):
    tokens_here = queries.shape[0]
    wide_count = lax.axis_size("wide")
    device_index = lax.axis_index("wide")
    local_places = jnp.arange(tokens_here, dtype=jnp.int32)
    query_places = device_index * tokens_here + local_places
    query_docs = doc_number(query_places, doc_lengths)
    query_images = image_number(device_index, local_places, image_count, image_offset)
    own_block = jnp.stack([keys, values])
    blocks = [own_block]
    moving = own_block
    for offset in range(REACH):
        moving = passed_along(moving, "wide", 1)
        blocks.append(moving)
    masks = []
    for offset in range(REACH + 1):
        source = (device_index - offset) % wide_count
        key_places = source * tokens_here + local_places
        key_docs = doc_number(key_places, doc_lengths)
        key_images = image_number(source, local_places, image_count, image_offset)
        visible = allowed_mask(
            query_places, query_docs, query_images, key_places, key_docs, key_images
        )
        masks.append(visible & (device_index - offset >= 0))
    allowed = jnp.concatenate(masks, axis=1)
    key_all = jnp.concatenate([block[0] for block in blocks], axis=0)
    value_all = jnp.concatenate([block[1] for block in blocks], axis=0)
    dquery, dkey, dvalue = attend_block(queries, key_all, value_all, out_grad, allowed)
    parts = [
        jnp.stack(
            [
                dkey[offset * tokens_here : (offset + 1) * tokens_here],
                dvalue[offset * tokens_here : (offset + 1) * tokens_here],
            ]
        )
        for offset in range(REACH + 1)
    ]
    carried = jnp.zeros_like(parts[0])
    for offset in range(REACH):
        carried = passed_along(carried + parts[REACH - offset], "wide", -1)
    key_grads = parts[0] + carried
    return jnp.stack(
        [
            dquery.astype(jnp.bfloat16),
            key_grads[0].astype(jnp.bfloat16),
            key_grads[1].astype(jnp.bfloat16),
        ]
    )
def tail_kernel(slab_ref, seg_ref, klow_ref, act_t, in_t, pre_ref, kern1, kern2, mean1, mean2, sq1, sq2,
                o_k1, o_k2, o_m1, o_m2, o_s1, o_s2,
                seg_all, klow_all, out_seg, seg_in, grads, grads_in, total_all, norm_all,
                sem_hs, sem_hr, sem_ks, sem_kr, sem_ss, sem_sr, sem_gs, sem_gr, sem_ts, sem_tr, sem_ns, sem_nr):
    heads, wide = seg_all.shape[0], klow_all.shape[0]
    me, head = lax.axis_index("wide"), lax.axis_index("head")
    slab = pre_ref.shape[0]
    send_rows = out_seg.shape[0]
    pad = klow_all.shape[1]
    chunk = kern1.shape[0]

    def go(axis, mine, count, source, dest, send, recv):
        def one(d, c):
            peer = lax.rem(mine + d, count)
            pltpu.make_async_remote_copy(
                src_ref=source(peer), dst_ref=dest.at[mine], send_sem=send.at[peer],
                recv_sem=recv.at[mine], device_id={axis: peer},
                device_id_type=pl.DeviceIdType.MESH,
            ).start()
            return c

        lax.fori_loop(1, count, one, 0)

    def done(axis, mine, count, source, dest, send, recv):
        def one(d, c):
            peer = lax.rem(mine + d, count)
            copy = pltpu.make_async_remote_copy(
                src_ref=source(peer), dst_ref=dest.at[peer], send_sem=send.at[peer],
                recv_sem=recv.at[peer], device_id={axis: peer},
                device_id_type=pl.DeviceIdType.MESH,
            )
            copy.wait_send()
            copy.wait_recv()
            return c

        lax.fori_loop(1, count, one, 0)

    barrier = pltpu.get_barrier_semaphore()

    def hello(axis, mine, count):
        def one(d, c):
            pl.semaphore_signal(barrier, inc=1, device_id={axis: lax.rem(mine + d, count)},
                                device_id_type=pl.DeviceIdType.MESH)
            return c

        lax.fori_loop(1, count, one, 0)

    hello("head", head, heads)
    hello("wide", me, wide)
    pl.semaphore_wait(barrier, heads + wide - 2)

    seg_all[head] = seg_ref[...]
    by_head = ("head", head, heads, lambda p: seg_all.at[head], seg_all, sem_hs, sem_hr)
    go(*by_head)
    klow_all[me] = klow_ref[...]
    by_kern = ("wide", me, wide, lambda p: klow_all.at[me], klow_all, sem_ks, sem_kr)
    go(*by_kern)
    done(*by_head)
    rows = pl.ds(pl.multiple_of(head * slab, 8), send_rows)
    seg = seg_all[0, rows]
    for h in range(1, heads):
        seg = seg + seg_all[h, rows]
    out_seg[...] = seg.astype(jnp.bfloat16)
    by_seg = ("wide", me, wide, lambda p: out_seg, seg_in, sem_ss, sem_sr)
    go(*by_seg)
    seg_in[me] = out_seg[...]
    done(*by_kern)
    cmid = pre_ref.shape[1]
    flat = klow_all[...].reshape(wide * pad, klow_all.shape[2])
    middle = chunk // 9
    row = lax.broadcasted_iota(jnp.int32, (cmid, wide * pad), 0)
    col = lax.broadcasted_iota(jnp.int32, (cmid, wide * pad), 1)
    place = row // middle * pad + row % middle * 9
    second = []
    for o in range(9):
        pick = (col == place + o).astype(jnp.float32).astype(jnp.bfloat16)
        second.append(
            jnp.dot(pick, flat, preferred_element_type=jnp.float32).astype(jnp.bfloat16)
        )
    done(*by_seg)
    incoming = jnp.zeros((send_rows, seg_in.shape[2]), jnp.float32)
    for n in range(wide):
        chosen = jnp.where(slab_ref[n] == me, 1.0, 0.0)
        incoming = incoming + seg_in[n].astype(jnp.float32) * chosen
    column = lax.broadcasted_iota(jnp.int32, incoming.shape, 0) % PCOLS
    shifted = [
        jnp.where(column < PCOLS - 1, pltpu.roll(incoming, send_rows - 1, 0), 0.0),
        incoming,
        jnp.where(column > 0, pltpu.roll(incoming, 1, 0), 0.0),
    ]
    dact = jnp.zeros((slab, cmid), jnp.float32)
    for o in range(9):
        start = PCOLS * (2 - o // 3)
        moved = shifted[o % 3][start : start + slab].astype(jnp.bfloat16)
        dact = dact + lax.dot_general(
            moved, second[o], (((1,), (1,)), ((), ())), preferred_element_type=jnp.float32
        )
    pre = pre_ref[...].astype(jnp.float32)
    sig = 1.0 / (1.0 + jnp.exp(-pre))
    dpre = (dact * sig * (1.0 + pre * (1.0 - sig))).astype(jnp.bfloat16)
    middle_in = incoming[PCOLS : PCOLS + slab].astype(jnp.bfloat16)
    width1 = dpre.shape[1]
    width2 = middle_in.shape[1]
    for w in range(wide):
        grads[w, :, :width1] = jnp.dot(
            in_t[w], dpre, preferred_element_type=jnp.float32
        ).astype(jnp.bfloat16)
        grads[w, :, width1:] = jnp.dot(
            act_t[w], middle_in, preferred_element_type=jnp.float32
        ).astype(jnp.bfloat16)
    by_grad = ("wide", me, wide, lambda p: grads.at[p], grads_in, sem_gs, sem_gr)
    go(*by_grad)
    grads_in[me] = grads[me]
    done(*by_grad)
    total = grads_in[0].astype(jnp.float32)
    for w in range(1, wide):
        total = total + grads_in[w].astype(jnp.float32)
    total_all[head] = total
    by_total = ("head", head, heads, lambda p: total_all.at[head], total_all, sem_ts, sem_tr)
    go(*by_total)
    done(*by_total)
    total = total_all[0]
    for h in range(1, heads):
        total = total + total_all[h]
    square = jnp.sum(total * total, axis=0, keepdims=True)
    square = jnp.sum(square, axis=1, keepdims=True)
    norm_all[me] = jnp.broadcast_to(square, norm_all.shape[1:])
    by_norm = ("wide", me, wide, lambda p: norm_all.at[me], norm_all, sem_ns, sem_nr)
    go(*by_norm)
    done(*by_norm)
    squares = norm_all[0]
    for w in range(1, wide):
        squares = squares + norm_all[w]
    squares = squares[:1, :1]
    limit = 0.5 * math.sqrt(wide * chunk * (width1 + width2))
    factor = jnp.minimum(1.0, limit / (jnp.sqrt(squares) + norm_eps))
    total = total * factor
    o_k1[...], o_m1[...], o_s1[...] = adam_update(
        kern1[...], mean1[...], sq1[...], total[:chunk, :width1]
    )
    o_k2[...], o_m2[...], o_s2[...] = adam_update(
        kern2[...], mean2[...], sq2[...], total[:chunk, width1:]
    )


def conv_update(seg, slab_owner, act, conv_input, pre_act, params):
    wide = lax.axis_size("wide")
    heads = lax.axis_size("head")
    slab_rows = pre_act.shape[1]
    slab = slab_rows * PCOLS
    kern1, kern2 = params[0], params[1]
    chunk = kern1.shape[0]
    pad = (chunk + 15) // 16 * 16
    send_rows = (slab + 2 * PCOLS + 15) // 16 * 16
    seg_rows = (heads - 1) * slab + send_rows
    seg = jnp.pad(seg, ((PCOLS, seg_rows - PCOLS - seg.shape[0]), (0, 0)))
    klow = jnp.pad(kern2.astype(jnp.bfloat16), ((0, pad - chunk), (0, 0)))
    both = with_halo(jnp.stack([conv_input, act]), (("head", 2),), 1)
    rims = jnp.pad(both, ((0, 0), (0, 0), (0, 0), (1, 1), (0, 0)))
    pieces = jnp.stack(
        [
            rims[:, 0, r : r + slab_rows, c : c + PCOLS].reshape(2, slab, -1)
            for r in range(3)
            for c in range(3)
        ],
        axis=1,
    )
    pieces = pieces.transpose(0, 3, 1, 2).reshape(2, wide, chunk, slab)
    pieces = jnp.pad(pieces, ((0, 0), (0, 0), (0, pad - chunk), (0, 0)))
    pch = kern2.shape[1]
    both_width = pch + kern1.shape[1]
    vmem = pl.BlockSpec(memory_space=pltpu.VMEM)
    dma = pltpu.SemaphoreType.DMA
    low, full = jnp.bfloat16, jnp.float32
    return pl.pallas_call(
        tail_kernel,
        in_specs=[pl.BlockSpec(memory_space=pltpu.SMEM)] + [vmem] * 11,
        out_specs=[vmem] * 6,
        out_shape=[jax.ShapeDtypeStruct(p.shape, p.dtype) for p in params],
        scratch_shapes=[
            pltpu.VMEM((heads, seg_rows, pch), full),
            pltpu.VMEM((wide, pad, pch), low),
            pltpu.VMEM((send_rows, pch), low),
            pltpu.VMEM((wide, send_rows, pch), low),
            pltpu.VMEM((wide, pad, both_width), low),
            pltpu.VMEM((wide, pad, both_width), low),
            pltpu.VMEM((heads, pad, both_width), full),
            pltpu.VMEM((wide, 8, 128), full),
        ]
        + [dma((n,)) for n in (heads, wide, wide, wide, heads, wide) for _ in range(2)],
        compiler_params=pltpu.CompilerParams(
            collective_id=0, has_side_effects=True, vmem_limit_bytes=32 * 1024 * 1024
        ),
        cost_estimate=pl.CostEstimate(
            flops=10**9, bytes_accessed=4 * 10**6, transcendentals=10**4
        ),
    )(slab_owner, seg, klow, pieces[1], pieces[0], pre_act.reshape(slab, -1), *params)


def shards(
    queries,
    keys,
    values,
    out_grad,
    qkv_weight,
    doc_lengths,
    image_count,
    image_offset,
    slab_owner,
    patch_weight,
    conv_input,
    pre_act,
    kernel_first,
    kernel_second,
    mean_first,
    mean_second,
    square_first,
    square_second,
):
    device_index = lax.axis_index("wide")
    heads_here = queries.shape[1] // HD
    wide_count = lax.axis_size("wide")
    split = heads_here % REACH == 0 and wide_count % REACH == 0
    grads = (attend_heads if split else attend_ring)(
        queries, keys, values, out_grad, doc_lengths, image_count, image_offset
    )
    weight = lax.all_gather(qkv_weight, "wide", axis=1, tiled=True)
    if lax.axis_size("head") == 2:
        half = weight.shape[1] // 2
        head_index = lax.axis_index("head")

        def features(owner):
            rows = lax.dynamic_slice_in_dim(weight, owner * half, half, axis=1)
            product = jnp.einsum("prk,ptk->rt", rows, grads, preferred_element_type=jnp.float32)
            return product.astype(jnp.bfloat16)

        arrived = lax.ppermute(features(1 - head_index), "head", [(0, 1), (1, 0)])
        own = lax.optimization_barrier(features(head_index))
        input_grad_t = (own.astype(jnp.float32) + arrived.astype(jnp.float32)).astype(jnp.bfloat16)
    else:
        partial_value = jnp.einsum(
            "prk,ptk->rt", weight, grads, preferred_element_type=jnp.float32
        ).astype(jnp.bfloat16)
        input_grad_t = lax.psum_scatter(partial_value, "head", scatter_dimension=0, tiled=True)
    patch_part = lax.dot_general(
        input_grad_t, patch_weight, (((0,), (1,)), ((), ())), preferred_element_type=jnp.float32
    )
    has_image = pick_entry(image_count, device_index)
    offset_here = pick_entry(image_offset, device_index)
    segment = lax.dynamic_slice_in_dim(patch_part, offset_here, IMGTOK, 0)
    segment = segment * has_image.astype(jnp.float32)
    act = jax.nn.silu(pre_act.astype(jnp.float32)).astype(jnp.bfloat16)
    updated = conv_update(
        segment,
        slab_owner,
        act,
        conv_input,
        pre_act,
        (kernel_first, kernel_second, mean_first, mean_second, square_first, square_second),
    )
    kernel_one, kernel_two, mean_one, mean_two, square_one, square_two = updated
    return (input_grad_t, kernel_one, kernel_two, mean_one, mean_two, square_one, square_two)


def solution(mesh):
    in_specs = (
        P("wide", "head"),
        P("wide", "head"),
        P("wide", "head"),
        P("wide", "head"),
        P(None, "wide", "head"),
        P(),
        P(),
        P(),
        P(),
        P(None, "head"),
        P("wide", "head", None, None),
        P("wide", "head", None, None),
        P("wide", None),
        P("wide", None),
        P("wide", None),
        P("wide", None),
        P("wide", None),
        P("wide", None),
    )
    out_specs = (
        P("head", "wide"),
        P("wide", None),
        P("wide", None),
        P("wide", None),
        P("wide", None),
        P("wide", None),
        P("wide", None),
    )
    return jax.shard_map(shards, mesh=mesh, in_specs=in_specs, out_specs=out_specs, check_vma=False)
```
